128 devices in a mesh: dp: 8 (over z, core), seq: 16 (over y, x).
Axes of the slice: x: 4, y: 4, z: 4, core: 2. Of those that a mesh axis runs over, the one named last changes fastest.
Arguments:
- query_heads: bfloat16 [8, 6144, 4096], P('dp', 'seq'), may hold values from -6 to 6
- key_heads: bfloat16 [8, 6144, 4096], P('dp', 'seq'), may hold values from -6 to 6
- value_heads: bfloat16 [8, 6144, 4096], P('dp', 'seq'), may hold values from -6 to 6
- output_grad: bfloat16 [8, 6144, 4096], P('dp', 'seq'), may hold values from -6 to 6
- layer_input: bfloat16 [8, 6144, 6144], P('dp', 'seq'), may hold values from -6 to 6
- gate_weight: bfloat16 [6144, 32], replicated, may hold values from -0.078125 to 0.078125
- decay_rate: float32 [8, 32, 6144], P('dp', None, 'seq'), may hold values from 0 to 0.3, as said below
Outputs:
- query_grad: bfloat16 [8, 6144, 4096], P('dp', 'seq')
- key_grad: bfloat16 [8, 6144, 4096], P('dp', 'seq')
- value_grad: bfloat16 [8, 6144, 4096], P('dp', 'seq')
- gate_weight_grad: float32 [32, 6144], P(None, 'seq')
The draws below stay inside these ranges and needn't reach their ends.
Inputs may be any that keep to these rules, and one draw needn't show every extreme that they name: `decay_rate`: positive rates.
All inputs are finite; a program needn't handle non-finite values.
Results may differ from the reference program's by a relative error of at most 0.009.
Values sent between devices are 32-bit elements; how exact they have to be, the bound alone decides.
No kernel may reach another device: no remote copies, remote signals or barrier semaphores. Data moves between devices by JAX's collectives and lax.ppermute only.
A program may use at most 256 MiB of HBM per device.

```python
import math
import jax
import jax.numpy as jnp
from jax import lax

HEAD_GROUP = 32
DH = 128
DM = 6144
TOK_DEV = 384
HD = 4096
SEQUENCE_LENGTH = 6144
SEQUENCE_COUNT = 8


def draw_decay_rate(key, part):
    key = jax.random.fold_in(key, 11)
    random_subkeys = jax.random.split(key, 7)
    blocks = SEQUENCE_LENGTH // TOK_DEV
    random_noise = jnp.exp(jax.random.uniform(random_subkeys[0], (SEQUENCE_COUNT, HEAD_GROUP, SEQUENCE_LENGTH), jnp.float32, -0.35, 0.35))
    slow_cut = 5
    slow_head = jax.random.randint(random_subkeys[1], (SEQUENCE_COUNT, HEAD_GROUP, 1), 0, 10) < slow_cut
    slow_rate = jnp.exp(jax.random.uniform(random_subkeys[2], (SEQUENCE_COUNT, HEAD_GROUP, 1), jnp.float32, math.log(0.03), math.log(0.15))) / SEQUENCE_LENGTH
    fast_rate = jnp.exp(jax.random.uniform(random_subkeys[3], (SEQUENCE_COUNT, HEAD_GROUP, 1), jnp.float32, math.log(1.0 / 50.0), math.log(1.0 / 30.0)))
    head_decay = jnp.where(slow_head, slow_rate, fast_rate)
    block_multiplier = jnp.exp(jax.random.uniform(random_subkeys[4], (SEQUENCE_COUNT, HEAD_GROUP, blocks, 1), jnp.float32, math.log(0.5), 0.0))
    block_multiplier = jnp.broadcast_to(block_multiplier, (SEQUENCE_COUNT, HEAD_GROUP, blocks, TOK_DEV)).reshape(SEQUENCE_COUNT, HEAD_GROUP, SEQUENCE_LENGTH)
    spike_position = jax.random.randint(random_subkeys[5], (SEQUENCE_COUNT, HEAD_GROUP, 3, 1), 0, SEQUENCE_LENGTH)
    token_position = jnp.arange(SEQUENCE_LENGTH)[None, None, None, :]
    spike_flag = jnp.any(token_position == spike_position, axis=2)
    spike_decay_rate = jax.random.uniform(random_subkeys[6], (SEQUENCE_COUNT, HEAD_GROUP, SEQUENCE_LENGTH), jnp.float32, 0.12, 0.3)
    return jnp.where(spike_flag, spike_decay_rate, head_decay * block_multiplier * random_noise)


def with_spikes(values, rng, source, target, shards_of, factor):
    def block_of(axis_at):
        return (jnp.arange(values.shape[axis_at]) // (values.shape[axis_at] // shards_of)).reshape((-1,) + (1,) * (values.ndim - 1 - axis_at))

    one_side = jax.random.permutation(rng, shards_of)[block_of(target)]
    second = (block_of(target) + shards_of // 2) % shards_of
    return jnp.where((block_of(source) == one_side) | (block_of(source) == second), factor * values, values)


def block_levels(rng, shape, pieces, least, top_value):
    factor_of, own = 1.0, jax.random.fold_in(rng, 6)
    for position, parts in pieces:
        steps = jnp.exp(jax.random.uniform(jax.random.fold_in(own, position), (parts,), jnp.float32, least / len(pieces), top_value / len(pieces)))
        factor_of = factor_of * jnp.repeat(steps, shape[position] // parts).reshape([-1 if axis == position else 1 for axis in range(len(shape))])
    return factor_of


def normal_values(key, shape, width, bound, cuts=(), held_as=jnp.bfloat16):
    result = width * jax.random.normal(key, shape, jnp.float32)
    if cuts:
        result = result * block_levels(key, shape, cuts, -0.22, 0.18)
    return jnp.clip(result, -bound, bound).astype(held_as)


def gaussian_with(rng, extent, scale, most, cuts, heavy, dtype=jnp.bfloat16):
    values = scale * jax.random.normal(rng, extent, jnp.float32)
    if cuts:
        values = values * block_levels(rng, extent, cuts, -0.22, 0.18)
    return jnp.clip(with_spikes(values, jax.random.fold_in(rng, 3), *heavy), -most, most).astype(dtype)


def setup_inputs(seed: int = 0) -> dict:
    arg_keys = jax.random.split(jax.random.key(seed), 8)
    query_heads = normal_values(arg_keys[0], (SEQUENCE_COUNT, SEQUENCE_LENGTH, HD), 1.0, 6.0, ((0, 8), (1, 16)))
    key_heads = normal_values(arg_keys[1], (SEQUENCE_COUNT, SEQUENCE_LENGTH, HD), 1.0, 6.0, ((0, 8), (1, 16)))
    value_heads = normal_values(arg_keys[2], (SEQUENCE_COUNT, SEQUENCE_LENGTH, HD), 1.0, 6.0, ((0, 8), (1, 16)))
    output_grad = normal_values(arg_keys[3], (SEQUENCE_COUNT, SEQUENCE_LENGTH, HD), 1.0, 6.0, ((0, 8), (1, 16)))
    layer_input = gaussian_with(arg_keys[4], (SEQUENCE_COUNT, SEQUENCE_LENGTH, DM), 1.0, 6.0, ((0, 8), (1, 16)), (1, 2, 16, 2.0))
    gate_weight = normal_values(arg_keys[5], (DM, HEAD_GROUP), DM ** -0.5, 0.078125)
    decay_rate = draw_decay_rate(jax.random.fold_in(arg_keys[7], 71), 0)
    return dict(query_heads=query_heads, key_heads=key_heads, value_heads=value_heads, output_grad=output_grad, layer_input=layer_input, gate_weight=gate_weight, decay_rate=decay_rate)


def round_low(values_in):
    return lax.optimization_barrier(values_in.astype(jnp.bfloat16)).astype(jnp.float32)


def fold_step(carried, block_item):
    fading, states = block_item
    return fading[:, None, None] * carried + states, carried


def local_part(block_item):
    query_rows, key_rows, value_rows, grad_rows, running, block_total = block_item
    token_position = jnp.arange(TOK_DEV)
    causal = (token_position[:, None] >= token_position[None, :])[None]
    log_gap = jnp.where(causal, running[:, :, None] - running[:, None, :], 0.0)
    decay_table = jnp.where(causal, jnp.exp(log_gap), 0.0) * (1.0 / DH)
    scores = jnp.einsum("thd,shd->hts", query_rows, key_rows)
    weighted = round_low(scores * decay_table)
    grad_scores = jnp.einsum("thd,shd->hts", grad_rows, value_rows)
    mixing = round_low(grad_scores * decay_table)
    query_local = jnp.einsum("hts,shd->thd", mixing, key_rows)
    key_local = jnp.einsum("hts,thd->shd", mixing, query_rows)
    value_local = jnp.einsum("hts,thd->shd", weighted, grad_rows)
    to_end = jnp.exp(block_total[:, None] - running).T[:, :, None]
    from_start = jnp.exp(running).T[:, :, None]
    key_faded = round_low(key_rows * to_end)
    query_faded = round_low(query_rows * from_start)
    states = jnp.einsum("thd,the->hde", key_faded, value_rows)
    grad_state = jnp.einsum("thd,the->hde", query_faded, grad_rows)
    return query_local, key_local, value_local, states, grad_state, to_end, from_start


def one_sequence(query_heads, key_heads, value_heads, output_grad, layer_input, gate_weight, decay_rate):
    blocks = SEQUENCE_LENGTH // TOK_DEV
    scale_factor = 1.0 / DH
    input_wide = layer_input.astype(jnp.float32)
    gate_open = jax.nn.sigmoid(jnp.dot(input_wide, gate_weight.astype(jnp.float32), preferred_element_type=jnp.float32).T)
    log_gate = -2.0 * decay_rate * gate_open
    running = jnp.cumsum(log_gate.reshape(HEAD_GROUP, blocks, TOK_DEV), axis=2).transpose(1, 0, 2)
    block_total = running[:, :, -1]

    def split_rows(array_in):
        return array_in.reshape(blocks, TOK_DEV, HEAD_GROUP, DH).astype(jnp.float32)

    query_rows = split_rows(query_heads)
    key_rows = split_rows(key_heads)
    value_rows = split_rows(value_heads)
    grad_rows = split_rows(output_grad)
    query_local, key_local, value_local, states, grad_state, to_end, from_start = lax.map(
        local_part, (query_rows, key_rows, value_rows, grad_rows, running, block_total))
    fading = jnp.exp(block_total)
    zero_state = jnp.zeros((HEAD_GROUP, DH, DH), jnp.float32)
    _, prior_state = lax.scan(fold_step, zero_state, (fading, states))
    _, later_state = lax.scan(fold_step, zero_state, (fading, grad_state), reverse=True)
    prior_low = round_low(prior_state)
    later_low = round_low(later_state)
    query_full = query_local + from_start * scale_factor * jnp.einsum("nthe,nhde->nthd", grad_rows, prior_low)
    key_full = key_local + to_end * scale_factor * jnp.einsum("nthe,nhde->nthd", value_rows, later_low)
    value_full = value_local + to_end * scale_factor * jnp.einsum("nthd,nhde->nthe", key_rows, later_low)
    gate_push = jnp.sum(query_rows * query_full - key_rows * key_full, axis=3).reshape(SEQUENCE_LENGTH, HEAD_GROUP).T
    gate_grad = jnp.cumsum(gate_push[:, ::-1], axis=1)[:, ::-1]
    logit_grad = round_low(gate_grad * log_gate * (1.0 - gate_open))
    gate_term = jnp.dot(logit_grad, input_wide, preferred_element_type=jnp.float32)
    return (query_full.reshape(SEQUENCE_LENGTH, HD).astype(jnp.bfloat16),
            key_full.reshape(SEQUENCE_LENGTH, HD).astype(jnp.bfloat16),
            value_full.reshape(SEQUENCE_LENGTH, HD).astype(jnp.bfloat16),
            gate_term)


def reference(query_heads, key_heads, value_heads, output_grad, layer_input, gate_weight, decay_rate):
    def per_sequence(items):
        return one_sequence(items[0], items[1], items[2], items[3], items[4], gate_weight, items[5])

    query_grad, key_grad, value_grad, gate_terms = lax.map(
        per_sequence, (query_heads, key_heads, value_heads, output_grad, layer_input, decay_rate))
    gate_weight_grad = jnp.sum(gate_terms, axis=0) / (SEQUENCE_COUNT * SEQUENCE_LENGTH)
    return query_grad, key_grad, value_grad, gate_weight_grad
```

```python
import jax
import jax.numpy as jnp
from jax import lax
from jax.experimental import pallas as pl
from jax.experimental.pallas import tpu as pltpu
from jax.sharding import PartitionSpec as P

F32 = jnp.float32
BF16 = jnp.bfloat16
BLOCK = 384
HEADS = 32
DIM = 128
MODEL = 6144
GROUPS = 16
PER = HEADS // GROUPS
WIDE = PER * DIM
SCALE = 1.0 / DIM
GATE_STEP = 1536
TERM_OWNERS = 2
LIMIT = pltpu.CompilerParams(vmem_limit_bytes=48 * 1024 * 1024)


def dot(a, b, dims):
    return lax.dot_general(a, b, (dims, ((), ())), preferred_element_type=F32)


def as_column(row):
    return jnp.broadcast_to(row, (DIM, BLOCK)).T


def row_sums(rows):
    ones = jnp.ones((8, DIM), BF16)
    high = rows.astype(BF16)
    low = (rows - high.astype(F32)).astype(BF16)
    both = dot(ones, high, ((1,), (1,))) + dot(ones, low, ((1,), (1,)))
    return both[0:1]


def gate_kernel(input_ref, weight_ref, rate_ref, running_ref, slope_ref, logits):
    step = pl.program_id(0)
    part = dot(input_ref[0], weight_ref[...], ((1,), (0,)))

    @pl.when(step == 0)
    def _():
        logits[...] = part

    @pl.when(step > 0)
    def _():
        logits[...] += part

    @pl.when(step == pl.num_programs(0) - 1)
    def _():
        gate_open = jax.nn.sigmoid(logits[...].T)
        log_gate = -2.0 * rate_ref[0] * gate_open
        first = lax.broadcasted_iota(jnp.int32, (BLOCK, BLOCK), 0)
        second = lax.broadcasted_iota(jnp.int32, (BLOCK, BLOCK), 1)
        upper = (first <= second).astype(F32)
        running_ref[...] = jnp.dot(
            log_gate, upper, precision=lax.Precision.HIGHEST, preferred_element_type=F32
        )
        slope_ref[...] = log_gate * (1.0 - gate_open)


def state_kernel(query_ref, key_ref, value_ref, grad_ref, running_ref, out_ref):
    fades = []
    for j in range(PER):
        cols = slice(j * DIM, (j + 1) * DIM)
        row = running_ref[0, j : j + 1, :]
        column = as_column(row)
        total = row[:, BLOCK - 1 : BLOCK]
        key_faded = (key_ref[0, :, cols].astype(F32) * jnp.exp(total - column)).astype(BF16)
        query_faded = (query_ref[0, :, cols].astype(F32) * jnp.exp(column)).astype(BF16)
        base = 2 * DIM * j
        out_ref[0, base : base + DIM, :] = dot(key_faded, value_ref[0, :, cols], ((0,), (0,)))
        out_ref[0, base + DIM : base + 2 * DIM, :] = dot(
            query_faded, grad_ref[0, :, cols], ((0,), (0,))
        )
        fades.append(jnp.broadcast_to(jnp.exp(total), (8, DIM)))
    place = lax.broadcasted_iota(jnp.int32, (8, DIM), 0)
    out_ref[0, 2 * DIM * PER :, :] = jnp.where(place == 0, fades[0], fades[1])


def scan_kernel(states_ref, fades_ref, out_ref):
    head = pl.program_id(0)
    out_ref[0, :DIM, :] = jnp.zeros((DIM, DIM), F32)
    out_ref[GROUPS - 1, DIM:, :] = jnp.zeros((DIM, DIM), F32)
    for n in range(GROUPS - 1):
        fade = fades_ref[n, pl.ds(head, 1), :]
        out_ref[n + 1, :DIM, :] = states_ref[n, :DIM, :] + fade * out_ref[n, :DIM, :]
        m = GROUPS - 1 - n
        fade = fades_ref[m, pl.ds(head, 1), :]
        out_ref[m - 1, DIM:, :] = states_ref[m, DIM:, :] + fade * out_ref[m, DIM:, :]


def local_kernel(
    query_ref, key_ref, value_ref, grad_ref, running_ref, ql_ref, kl_ref, vl_ref, push_ref
):
    first = lax.broadcasted_iota(jnp.int32, (BLOCK, BLOCK), 0)
    second = lax.broadcasted_iota(jnp.int32, (BLOCK, BLOCK), 1)
    causal = first >= second
    for j in range(PER):
        cols = slice(j * DIM, (j + 1) * DIM)
        row = running_ref[0, j : j + 1, :]
        column = jnp.broadcast_to(row, (DIM, BLOCK)).T
        column = jnp.concatenate([column] * (BLOCK // DIM), axis=1)
        decay = jnp.exp(jnp.where(causal, column - row, -1e30)) * SCALE
        query, key = query_ref[0, :, cols], key_ref[0, :, cols]
        value, grad = value_ref[0, :, cols], grad_ref[0, :, cols]
        weighted = (dot(query, key, ((1,), (1,))) * decay).astype(BF16)
        mixing = (dot(grad, value, ((1,), (1,))) * decay).astype(BF16)
        query_local = dot(mixing, key, ((1,), (0,)))
        key_local = dot(mixing, query, ((0,), (0,)))
        ql_ref[:, cols] = query_local
        kl_ref[:, cols] = key_local
        vl_ref[:, cols] = dot(weighted, grad, ((0,), (0,)))
        push_ref[0, j : j + 1, :] = row_sums(
            query.astype(F32) * query_local - key.astype(F32) * key_local
        )


def push_kernel(
    query_ref, key_ref, value_ref, grad_ref, running_ref, carried_ref, local_ref, push_ref
):
    last = lax.broadcasted_iota(jnp.int32, (1, BLOCK), 1) == BLOCK - 1
    for j in range(PER):
        cols = slice(j * DIM, (j + 1) * DIM)
        base = 2 * DIM * j
        row = running_ref[0, j : j + 1, :]
        column = as_column(row)
        total = row[:, BLOCK - 1 : BLOCK]
        prior = carried_ref[0, base : base + DIM, :]
        later = carried_ref[0, base + DIM : base + 2 * DIM, :]
        query_state = dot(grad_ref[0, :, cols], prior.astype(BF16), ((1,), (1,)))
        key_state = dot(value_ref[0, :, cols], later.astype(BF16), ((1,), (1,)))
        from_query = query_ref[0, :, cols].astype(F32) * query_state * (jnp.exp(column) * SCALE)
        from_key = (
            key_ref[0, :, cols].astype(F32) * key_state * (jnp.exp(total - column) * SCALE)
        )
        crossing = jnp.sum(from_key, axis=0, keepdims=True) + (
            jnp.exp(total) * SCALE
        ) * jnp.sum(prior * later, axis=0, keepdims=True)
        tail = jnp.sum(crossing, axis=1, keepdims=True)
        push = row_sums(from_query - from_key) + local_ref[0, j : j + 1, :]
        push_ref[0, j : j + 1, :] = push + jnp.where(last, tail, 0.0)


def term_kernel(push_ref, slope_ref, input_ref, out_ref, logit_grad):
    @pl.when(pl.program_id(0) == 0)
    def _():
        first = lax.broadcasted_iota(jnp.int32, (BLOCK, BLOCK), 0)
        second = lax.broadcasted_iota(jnp.int32, (BLOCK, BLOCK), 1)
        lower = (first >= second).astype(F32)
        gate_grad = jnp.dot(
            push_ref[...], lower, precision=lax.Precision.HIGHEST, preferred_element_type=F32
        )
        logit_grad[...] = (gate_grad * slope_ref[...]).astype(BF16)

    for i in range(TERM_OWNERS):
        cols = slice(i * BLOCK, (i + 1) * BLOCK)
        out_ref[i] = dot(logit_grad[...], input_ref[0, :, cols], ((1,), (0,)))


def full_kernel(
    key_ref, value_ref, grad_ref, running_ref, carried_ref, ql_ref, kl_ref, vl_ref,
    query_out, key_out, value_out,
):
    for j in range(PER):
        cols = slice(j * DIM, (j + 1) * DIM)
        base = 2 * DIM * j
        row = running_ref[0, j : j + 1, :]
        column = as_column(row)
        total = row[:, BLOCK - 1 : BLOCK]
        from_start = jnp.exp(column) * SCALE
        to_end = jnp.exp(total - column) * SCALE
        prior = carried_ref[0, base : base + DIM, :].astype(BF16)
        later = carried_ref[0, base + DIM : base + 2 * DIM, :].astype(BF16)
        query_out[0, :, cols] = (
            ql_ref[:, cols] + from_start * dot(grad_ref[0, :, cols], prior, ((1,), (1,)))
        ).astype(BF16)
        key_out[0, :, cols] = (
            kl_ref[:, cols] + to_end * dot(value_ref[0, :, cols], later, ((1,), (1,)))
        ).astype(BF16)
        value_out[0, :, cols] = (
            vl_ref[:, cols] + to_end * dot(key_ref[0, :, cols], later, ((1,), (0,)))
        ).astype(BF16)


def heads_block():
    return pl.BlockSpec((1, BLOCK, WIDE), lambda i: (0, 0, i))


def rows_block():
    return pl.BlockSpec((1, PER, BLOCK), lambda i: (i, 0, 0))


def flat_block():
    return pl.BlockSpec((BLOCK, WIDE), lambda i: (0, i))


def local(query_heads, key_heads, value_heads, output_grad, layer_input, gate_weight, decay_rate):
    shape = jax.ShapeDtypeStruct
    rows = 2 * DIM * PER
    whole = pl.BlockSpec((HEADS, BLOCK), lambda i: (0, 0))
    running, slope = pl.pallas_call(
        gate_kernel,
        grid=(MODEL // GATE_STEP,),
        in_specs=[
            pl.BlockSpec((1, BLOCK, GATE_STEP), lambda i: (0, 0, i)),
            pl.BlockSpec((GATE_STEP, HEADS), lambda i: (i, 0)),
            pl.BlockSpec((1, HEADS, BLOCK), lambda i: (0, 0, 0)),
        ],
        out_specs=[whole, whole],
        out_shape=[shape((HEADS, BLOCK), F32)] * 2,
        scratch_shapes=[pltpu.VMEM((BLOCK, HEADS), F32)],
        compiler_params=LIMIT,
        name="gates",
    )(layer_input, gate_weight, decay_rate)
    running = running.reshape(GROUPS, PER, BLOCK)
    carried_block = pl.BlockSpec((1, rows, DIM), lambda i: (i, 0, 0))
    states = pl.pallas_call(
        state_kernel,
        grid=(GROUPS,),
        in_specs=[heads_block()] * 4 + [rows_block()],
        out_specs=pl.BlockSpec((1, rows + 8, DIM), lambda i: (i, 0, 0)),
        out_shape=shape((GROUPS, rows + 8, DIM), F32),
        compiler_params=LIMIT,
        name="states",
    )(query_heads, key_heads, value_heads, output_grad, running)
    states = lax.all_to_all(states, "seq", 0, 0, tiled=True)
    query_local, key_local, value_local, local_push = pl.pallas_call(
        local_kernel,
        grid=(GROUPS,),
        in_specs=[heads_block()] * 4 + [rows_block()],
        out_specs=[flat_block()] * 3 + [rows_block()],
        out_shape=[shape((BLOCK, HEADS * DIM), F32)] * 3 + [shape((GROUPS, PER, BLOCK), F32)],
        compiler_params=LIMIT,
        name="locals",
    )(query_heads, key_heads, value_heads, output_grad, running)
    carried = pl.pallas_call(
        scan_kernel,
        grid=(PER,),
        in_specs=[
            pl.BlockSpec((GROUPS, 2 * DIM, DIM), lambda i: (0, i, 0)),
            pl.BlockSpec((GROUPS, 8, DIM), lambda i: (0, rows // 8, 0)),
        ],
        out_specs=pl.BlockSpec((GROUPS, 2 * DIM, DIM), lambda i: (0, i, 0)),
        out_shape=shape((GROUPS, rows, DIM), F32),
        compiler_params=LIMIT,
        name="scan",
    )(states, states)
    carried = lax.all_to_all(carried, "seq", 0, 0, tiled=True)
    push = pl.pallas_call(
        push_kernel,
        grid=(GROUPS,),
        in_specs=[heads_block()] * 4 + [rows_block(), carried_block, rows_block()],
        out_specs=rows_block(),
        out_shape=shape((GROUPS, PER, BLOCK), F32),
        compiler_params=LIMIT,
        name="push",
    )(query_heads, key_heads, value_heads, output_grad, running, carried, local_push)
    terms = pl.pallas_call(
        term_kernel,
        grid=(GROUPS // TERM_OWNERS,),
        in_specs=[
            whole,
            whole,
            pl.BlockSpec((1, BLOCK, TERM_OWNERS * BLOCK), lambda i: (0, 0, i)),
        ],
        out_specs=pl.BlockSpec((TERM_OWNERS, HEADS, BLOCK), lambda i: (i, 0, 0)),
        out_shape=shape((GROUPS, HEADS, BLOCK), F32),
        scratch_shapes=[pltpu.VMEM((HEADS, BLOCK), BF16)],
        compiler_params=LIMIT,
        name="terms",
    )(push.reshape(HEADS, BLOCK), slope, layer_input)
    terms = jnp.sum(lax.all_to_all(terms, "seq", 0, 0, tiled=True), axis=0)
    query_grad, key_grad, value_grad = pl.pallas_call(
        full_kernel,
        grid=(GROUPS,),
        in_specs=[heads_block()] * 3 + [rows_block(), carried_block] + [flat_block()] * 3,
        out_specs=[heads_block()] * 3,
        out_shape=[shape((1, BLOCK, HEADS * DIM), BF16)] * 3,
        compiler_params=LIMIT,
        name="full",
    )(
        key_heads, value_heads, output_grad, running, carried,
        query_local, key_local, value_local,
    )
    token_count = BLOCK * lax.axis_size("seq") * lax.axis_size("dp")
    weight_grad = jnp.sum(lax.all_gather(terms, "dp"), axis=0) / token_count
    return query_grad, key_grad, value_grad, weight_grad


def solution(mesh):
    heads = P("dp", "seq", None)
    return jax.shard_map(
        local,
        mesh=mesh,
        in_specs=(heads,) * 5 + (P(), P("dp", None, "seq")),
        out_specs=(heads,) * 3 + (P(None, "seq"),),
        check_vma=False,
    )
```

```python
import jax
import jax.numpy as jnp
from jax import lax
from jax.experimental import pallas as pl
from jax.experimental.pallas import tpu as pltpu
from jax.sharding import PartitionSpec as P

F32 = jnp.float32
BF16 = jnp.bfloat16
BLOCK = 384
HEADS = 32
DIM = 128
MODEL = 6144
GROUPS = 16
PER = HEADS // GROUPS
ROWS = 2 * DIM + 8
SCALE = 1.0 / DIM
GATE_STEP = 3072
GATE_STEPS = MODEL // GATE_STEP
STATE_HEADS = 8
LOCAL_HEADS = 2
TERM_HEADS = 8
TERM_STEPS = HEADS // TERM_HEADS
FULL_HEADS = 8
TERM_OWNERS = 8
SCAN_MIB, TERM_MIB, FULL_MIB = 60, 60, 60


def limit(mib):
    return pltpu.CompilerParams(vmem_limit_bytes=mib * 1024 * 1024)


def dot(a, b, dims):
    return lax.dot_general(a, b, (dims, ((), ())), preferred_element_type=F32)


def rounded_sum(rounded, other):
    return jnp.sum(rounded.astype(BF16).astype(F32) * other, axis=0, keepdims=True) * SCALE


def as_column(row):
    return jnp.broadcast_to(row, (DIM, BLOCK)).T


def row_sums(rows):
    ones = jnp.ones((8, DIM), BF16)
    high = rows.astype(BF16)
    low = (rows - high.astype(F32)).astype(BF16)
    both = dot(ones, high, ((1,), (1,))) + dot(ones, low, ((1,), (1,)))
    return both[0:1]


def state_kernel(
    input_ref, weight_ref, rate_ref, query_ref, key_ref, value_ref, grad_ref,
    running_ref, slope_ref, decay_ref, out_ref, logits,
):
    step = pl.program_id(0)

    @pl.when(step == 0)
    def _():
        logits[...] = dot(weight_ref[...], input_ref[0], ((1,), (1,)))

    @pl.when((step > 0) & (step < GATE_STEPS))
    def _():
        logits[...] += dot(weight_ref[...], input_ref[0], ((1,), (1,)))

    @pl.when(step == GATE_STEPS - 1)
    def _():
        gate_open = jax.nn.sigmoid(logits[...])
        log_gate = -2.0 * rate_ref[0] * gate_open
        first = lax.broadcasted_iota(jnp.int32, (BLOCK, BLOCK), 0)
        second = lax.broadcasted_iota(jnp.int32, (BLOCK, BLOCK), 1)
        upper = (first <= second).astype(F32)
        running = jnp.dot(
            log_gate, upper, precision=lax.Precision.HIGHEST, preferred_element_type=F32
        )
        running_ref[...] = running
        slope_ref[...] = log_gate * (1.0 - gate_open)
        decay_ref[:HEADS, :] = jnp.exp(running)
        decay_ref[HEADS:, :] = jnp.exp(running[:, BLOCK - 1 : BLOCK] - running)

    @pl.when(step >= GATE_STEPS)
    def _():
        for j in range(STATE_HEADS):
            cols = slice(j * DIM, (j + 1) * DIM)
            head = (step - GATE_STEPS) * STATE_HEADS + j
            from_start = decay_ref[pl.ds(head, 1), :]
            to_end = decay_ref[pl.ds(HEADS + head, 1), :]
            key_faded = (key_ref[0, :, cols].T.astype(F32) * to_end).astype(BF16)
            query_faded = (query_ref[0, :, cols].T.astype(F32) * from_start).astype(BF16)
            out_ref[j, :DIM, :] = dot(key_faded, value_ref[0, :, cols], ((1,), (0,)))
            out_ref[j, DIM : 2 * DIM, :] = dot(query_faded, grad_ref[0, :, cols], ((1,), (0,)))
            out_ref[j, 2 * DIM :, :] = jnp.broadcast_to(
                from_start[:, BLOCK - 1 : BLOCK], (8, DIM)
            )


def scan_kernel(states_ref, out_ref):
    early, late, own = slice(0, DIM), slice(DIM, 2 * DIM), slice(2 * DIM, 2 * DIM + 1)
    prior = jnp.zeros((DIM, DIM), F32)
    pushes = []
    for n in range(GROUPS):
        out_ref[n, :DIM, :] = prior
        pushes.append(rounded_sum(prior, states_ref[n, late, :]))
        prior = states_ref[n, early, :] + states_ref[n, own, :] * prior
    later = jnp.zeros((DIM, DIM), F32)
    tail = jnp.zeros((1, DIM), F32)
    for n in reversed(range(GROUPS)):
        out_ref[n, DIM : 2 * DIM, :] = later
        out_ref[n, 2 * DIM :, :] = jnp.broadcast_to(tail, (8, DIM))
        tail = tail + pushes[n] - rounded_sum(later, states_ref[n, early, :])
        later = states_ref[n, late, :] + states_ref[n, own, :] * later


def local_kernel(
    query_ref, key_ref, value_ref, grad_ref, running_ref,
    ql_ref, kl_ref, vl_ref, qt_ref, kt_ref, push_ref,
):
    first = lax.broadcasted_iota(jnp.int32, (BLOCK, BLOCK), 0)
    second = lax.broadcasted_iota(jnp.int32, (BLOCK, BLOCK), 1)
    causal = first >= second
    for j in range(LOCAL_HEADS):
        cols = slice(j * DIM, (j + 1) * DIM)
        head = pl.ds(pl.program_id(0) * LOCAL_HEADS + j, 1)
        row = running_ref[head, :]
        column = jnp.concatenate([as_column(row)] * (BLOCK // DIM), axis=1)
        decay = jnp.exp(jnp.where(causal, column - row, -1e30)) * SCALE
        query, key = query_ref[0, :, cols], key_ref[0, :, cols]
        value, grad = value_ref[0, :, cols], grad_ref[0, :, cols]
        weighted = (dot(query, key, ((1,), (1,))) * decay).astype(BF16)
        mixing = (dot(grad, value, ((1,), (1,))) * decay).astype(BF16)
        query_local = dot(mixing, key, ((1,), (0,)))
        key_local = dot(mixing, query, ((0,), (0,)))
        qt_ref[cols, :] = query.T
        kt_ref[cols, :] = key.T
        ql_ref[:, cols] = query_local
        kl_ref[:, cols] = key_local
        vl_ref[:, cols] = dot(weighted, grad, ((0,), (0,)))
        push_ref[head, :] = row_sums(
            query.astype(F32) * query_local - key.astype(F32) * key_local
        )


def term_kernel(
    query_ref, key_ref, value_ref, grad_ref, decay_ref, carried_ref, local_ref, slope_ref,
    input_ref, out_ref, push,
):
    step = pl.program_id(0)

    @pl.when(step < TERM_STEPS)
    def _():
        last = lax.broadcasted_iota(jnp.int32, (1, BLOCK), 1) == BLOCK - 1
        for j in range(TERM_HEADS):
            head = step * TERM_HEADS + j
            cols = slice(j * DIM, (j + 1) * DIM)
            prior = carried_ref[j, :DIM, :].astype(BF16)
            later = carried_ref[j, DIM : 2 * DIM, :].astype(BF16)
            query_state = dot(prior, grad_ref[0, :, cols], ((1,), (1,)))
            key_state = dot(later, value_ref[0, :, cols], ((1,), (1,)))
            from_query = jnp.sum(
                query_ref[cols, :].astype(F32) * query_state, axis=0, keepdims=True
            ) * (decay_ref[pl.ds(head, 1), :] * SCALE)
            from_key = jnp.sum(
                key_ref[cols, :].astype(F32) * key_state, axis=0, keepdims=True
            ) * (decay_ref[pl.ds(HEADS + head, 1), :] * SCALE)
            tail = jnp.sum(carried_ref[j, 2 * DIM : 2 * DIM + 1, :], axis=1, keepdims=True)
            push[pl.ds(head, 1), :] = (
                from_query - from_key + local_ref[pl.ds(head, 1), :] + jnp.where(last, tail, 0.0)
            )

    @pl.when(step == TERM_STEPS - 1)
    def _():
        first = lax.broadcasted_iota(jnp.int32, (BLOCK, BLOCK), 0)
        second = lax.broadcasted_iota(jnp.int32, (BLOCK, BLOCK), 1)
        lower = (first >= second).astype(F32)
        gate_grad = jnp.dot(
            push[...], lower, precision=lax.Precision.HIGHEST, preferred_element_type=F32
        )
        push[...] = gate_grad * slope_ref[...]

    @pl.when(step >= TERM_STEPS)
    def _():
        logit_grad = push[...].astype(BF16)
        for i in range(TERM_OWNERS):
            cols = slice(i * BLOCK, (i + 1) * BLOCK)
            out_ref[i] = dot(logit_grad, input_ref[0, :, cols], ((1,), (0,)))


def query_kernel(
    value_ref, grad_ref, decay_ref, carried_ref, ql_ref, kl_ref, query_out, key_out
):
    for j in range(FULL_HEADS):
        cols = slice(j * DIM, (j + 1) * DIM)
        head = pl.program_id(0) * FULL_HEADS + j
        from_start = as_column(decay_ref[pl.ds(head, 1), :] * SCALE)
        to_end = as_column(decay_ref[pl.ds(HEADS + head, 1), :] * SCALE)
        prior = carried_ref[j, :DIM, :].astype(BF16)
        later = carried_ref[j, DIM : 2 * DIM, :].astype(BF16)
        query_out[0, :, cols] = (
            ql_ref[:, cols] + from_start * dot(grad_ref[0, :, cols], prior, ((1,), (1,)))
        ).astype(BF16)
        key_out[0, :, cols] = (
            kl_ref[:, cols] + to_end * dot(value_ref[0, :, cols], later, ((1,), (1,)))
        ).astype(BF16)


def value_kernel(key_ref, decay_ref, carried_ref, vl_ref, value_out):
    for j in range(FULL_HEADS):
        cols = slice(j * DIM, (j + 1) * DIM)
        head = pl.program_id(0) * FULL_HEADS + j
        to_end = as_column(decay_ref[pl.ds(HEADS + head, 1), :] * SCALE)
        later = carried_ref[j, DIM : 2 * DIM, :].astype(BF16)
        value_out[0, :, cols] = (
            vl_ref[:, cols] + to_end * dot(key_ref[0, :, cols], later, ((1,), (0,)))
        ).astype(BF16)


def same(i):
    return i


def heads_block(heads, group=same):
    return pl.BlockSpec((1, BLOCK, heads * DIM), lambda i: (0, 0, group(i)))


def carried_block(heads, group=same):
    return pl.BlockSpec((heads, ROWS, DIM), lambda i: (group(i), 0, 0))


def flat_block(heads, group=same):
    return pl.BlockSpec((BLOCK, heads * DIM), lambda i: (0, group(i)))


def turned_block(heads, group=same):
    return pl.BlockSpec((heads * DIM, BLOCK), lambda i: (group(i), 0))


def whole_block(*dims):
    return pl.BlockSpec(dims, lambda i: (0,) * len(dims))


shape = jax.ShapeDtypeStruct
ROW_TABLE = (HEADS, BLOCK)
DECAY_TABLE = (2 * HEADS, BLOCK)
TRAVELLING = (HEADS, ROWS, DIM)
OUT = (1, BLOCK, HEADS * DIM)


def states_of(layer_input, gate_weight, decay_rate, *heads):
    def feature(i):
        return jnp.minimum(i, GATE_STEPS - 1)

    def behind(i):
        return jnp.maximum(i - GATE_STEPS, 0)

    return pl.pallas_call(
        state_kernel,
        grid=(GATE_STEPS + HEADS // STATE_HEADS,),
        in_specs=[
            pl.BlockSpec((1, BLOCK, GATE_STEP), lambda i: (0, 0, feature(i))),
            pl.BlockSpec((HEADS, GATE_STEP), lambda i: (0, feature(i))),
            whole_block(1, HEADS, BLOCK),
        ]
        + [heads_block(STATE_HEADS, behind)] * 4,
        out_specs=[whole_block(*ROW_TABLE)] * 2
        + [whole_block(*DECAY_TABLE), carried_block(STATE_HEADS, behind)],
        out_shape=[shape(ROW_TABLE, F32)] * 2
        + [shape(DECAY_TABLE, F32), shape(TRAVELLING, F32)],
        scratch_shapes=[pltpu.VMEM(ROW_TABLE, F32)],
        compiler_params=limit(60),
        name="states",
    )(layer_input, gate_weight.T, decay_rate, *heads)


def locals_of(running, *heads):
    return pl.pallas_call(
        local_kernel,
        grid=(HEADS // LOCAL_HEADS,),
        in_specs=[heads_block(LOCAL_HEADS)] * 4 + [whole_block(*ROW_TABLE)],
        out_specs=[flat_block(LOCAL_HEADS)] * 3
        + [turned_block(LOCAL_HEADS)] * 2
        + [whole_block(*ROW_TABLE)],
        out_shape=[shape((BLOCK, HEADS * DIM), F32)] * 3
        + [shape((HEADS * DIM, BLOCK), BF16)] * 2
        + [shape(ROW_TABLE, F32)],
        compiler_params=limit(60),
        name="locals",
    )(*heads, running)


def scanned(states):
    return pl.pallas_call(
        scan_kernel,
        grid=(PER,),
        in_specs=[pl.BlockSpec((GROUPS, ROWS, DIM), lambda i: (0, i, 0))],
        out_specs=pl.BlockSpec((GROUPS, ROWS, DIM), lambda i: (0, i, 0)),
        out_shape=shape((GROUPS, PER * ROWS, DIM), F32),
        compiler_params=limit(SCAN_MIB),
        name="scan",
    )(states)


def exchanged(array, axis="seq"):
    return lax.all_to_all(array, axis, 0, 0, tiled=True)


def terms_of(turned, pair, decay, carried, local_push, slope, layer_input):
    def ahead(i):
        return jnp.minimum(i, TERM_STEPS - 1)

    def beyond(i):
        return jnp.maximum(i - TERM_STEPS, 0)

    return pl.pallas_call(
        term_kernel,
        grid=(TERM_STEPS + GROUPS // TERM_OWNERS,),
        in_specs=[turned_block(TERM_HEADS, ahead)] * 2
        + [heads_block(TERM_HEADS, ahead)] * 2
        + [
            whole_block(*DECAY_TABLE),
            carried_block(TERM_HEADS, ahead),
            whole_block(*ROW_TABLE),
            whole_block(*ROW_TABLE),
            pl.BlockSpec((1, BLOCK, TERM_OWNERS * BLOCK), lambda i: (0, 0, beyond(i))),
        ],
        out_specs=pl.BlockSpec((TERM_OWNERS, HEADS, BLOCK), lambda i: (beyond(i), 0, 0)),
        out_shape=shape((GROUPS, HEADS, BLOCK), F32),
        scratch_shapes=[pltpu.VMEM(ROW_TABLE, F32)],
        compiler_params=limit(TERM_MIB),
        name="terms",
    )(*turned, *pair, decay, carried, local_push, slope, layer_input)


def query_key(value_heads, output_grad, decay, carried, query_local, key_local):
    return pl.pallas_call(
        query_kernel,
        grid=(HEADS // FULL_HEADS,),
        in_specs=[heads_block(FULL_HEADS)] * 2
        + [whole_block(*DECAY_TABLE), carried_block(FULL_HEADS)]
        + [flat_block(FULL_HEADS)] * 2,
        out_specs=[heads_block(FULL_HEADS)] * 2,
        out_shape=[shape(OUT, BF16)] * 2,
        compiler_params=limit(FULL_MIB),
        name="query_key",
    )(value_heads, output_grad, decay, carried, query_local, key_local)


def value_of(key_heads, decay, carried, value_local):
    return pl.pallas_call(
        value_kernel,
        grid=(HEADS // FULL_HEADS,),
        in_specs=[
            heads_block(FULL_HEADS),
            whole_block(*DECAY_TABLE),
            carried_block(FULL_HEADS),
            flat_block(FULL_HEADS),
        ],
        out_specs=heads_block(FULL_HEADS),
        out_shape=shape(OUT, BF16),
        compiler_params=limit(FULL_MIB),
        name="value",
    )(key_heads, decay, carried, value_local)


def after(array, *others):
    return lax.optimization_barrier((array, *others))[0]


def local(query_heads, key_heads, value_heads, output_grad, layer_input, gate_weight, decay_rate):
    heads = (query_heads, key_heads, value_heads, output_grad)
    running, slope, decay, states = states_of(layer_input, gate_weight, decay_rate, *heads)
    owned = exchanged(states.reshape(GROUPS, PER * ROWS, DIM))
    carried = exchanged(scanned(owned)).reshape(TRAVELLING)
    query_local, key_local, value_local, query_turned, key_turned, local_push = locals_of(
        running, *heads
    )
    pair = (value_heads, output_grad)
    terms = exchanged(
        terms_of((query_turned, key_turned), pair, decay, carried, local_push, slope, layer_input)
    )
    query_grad, key_grad = query_key(*pair, decay, carried, query_local, key_local)
    sums = jnp.sum(terms, axis=0)
    value_local = after(value_local, sums)
    sums = after(sums, query_grad)
    copies = jnp.broadcast_to(sums[None], (lax.axis_size("dp"),) + sums.shape)
    gathered = exchanged(copies, "dp")
    value_grad = value_of(key_heads, decay, carried, value_local)
    token_count = BLOCK * lax.axis_size("seq") * lax.axis_size("dp")
    weight_grad = jnp.sum(gathered, axis=0) / token_count
    return query_grad, key_grad, value_grad, weight_grad


def solution(mesh):
    heads = P("dp", "seq", None)
    return jax.shard_map(
        local,
        mesh=mesh,
        in_specs=(heads,) * 5 + (P(), P("dp", None, "seq")),
        out_specs=(heads,) * 3 + (P(None, "seq"),),
        check_vma=False,
    )
```

```python
import jax
import jax.numpy as jnp
from jax import lax
from jax.experimental import pallas as pl
from jax.experimental.pallas import tpu as pltpu
from jax.sharding import PartitionSpec as P

F32 = jnp.float32
BF16 = jnp.bfloat16
BLOCK = 384
HEADS = 32
DIM = 128
MODEL = 6144
GROUPS = 16
PER = HEADS // GROUPS
ROWS = 2 * DIM * PER + 8
SCALE = 1.0 / DIM
GATE_STEP = 3072
GATE_STEPS = MODEL // GATE_STEP
STATE_HEADS = 8
LOCAL_HEADS = 2
TERM_HEADS = 8
TERM_STEPS = HEADS // TERM_HEADS
FULL_HEADS = 8
TERM_OWNERS = 8


def limit(mib):
    return pltpu.CompilerParams(vmem_limit_bytes=mib * 1024 * 1024)


def dot(a, b, dims):
    return lax.dot_general(a, b, (dims, ((), ())), preferred_element_type=F32)


def rounded_sum(rounded, other):
    return jnp.sum(rounded.astype(BF16).astype(F32) * other, axis=0, keepdims=True) * SCALE


def as_column(row):
    return jnp.broadcast_to(row, (DIM, BLOCK)).T


def row_sums(rows):
    ones = jnp.ones((8, DIM), BF16)
    high = rows.astype(BF16)
    low = (rows - high.astype(F32)).astype(BF16)
    both = dot(ones, high, ((1,), (1,))) + dot(ones, low, ((1,), (1,)))
    return both[0:1]


def travelling(head):
    base = 2 * DIM * (head % PER)
    own = 2 * DIM * PER + head % PER
    return (
        head // PER,
        slice(base, base + DIM),
        slice(base + DIM, base + 2 * DIM),
        slice(own, own + 1),
    )


def state_kernel(
    input_ref, weight_ref, rate_ref, query_ref, key_ref, value_ref, grad_ref,
    running_ref, slope_ref, decay_ref, out_ref, logits,
):
    step = pl.program_id(0)

    @pl.when(step == 0)
    def _():
        logits[...] = dot(weight_ref[...], input_ref[0], ((1,), (1,)))

    @pl.when((step > 0) & (step < GATE_STEPS))
    def _():
        logits[...] += dot(weight_ref[...], input_ref[0], ((1,), (1,)))

    @pl.when(step == GATE_STEPS - 1)
    def _():
        gate_open = jax.nn.sigmoid(logits[...])
        log_gate = -2.0 * rate_ref[0] * gate_open
        first = lax.broadcasted_iota(jnp.int32, (BLOCK, BLOCK), 0)
        second = lax.broadcasted_iota(jnp.int32, (BLOCK, BLOCK), 1)
        upper = (first <= second).astype(F32)
        running = jnp.dot(
            log_gate, upper, precision=lax.Precision.HIGHEST, preferred_element_type=F32
        )
        running_ref[...] = running
        slope_ref[...] = log_gate * (1.0 - gate_open)
        decay_ref[:HEADS, :] = jnp.exp(running)
        decay_ref[HEADS:, :] = jnp.exp(running[:, BLOCK - 1 : BLOCK] - running)

    @pl.when(step >= GATE_STEPS)
    def _():
        out_ref[:, 2 * DIM * PER :, :] = jnp.zeros((STATE_HEADS // PER, 8, DIM), F32)
        for j in range(STATE_HEADS):
            cols = slice(j * DIM, (j + 1) * DIM)
            head = (step - GATE_STEPS) * STATE_HEADS + j
            from_start = decay_ref[pl.ds(head, 1), :]
            to_end = decay_ref[pl.ds(HEADS + head, 1), :]
            key_faded = (key_ref[0, :, cols].T.astype(F32) * to_end).astype(BF16)
            query_faded = (query_ref[0, :, cols].T.astype(F32) * from_start).astype(BF16)
            at, early, late, own = travelling(j)
            out_ref[at, early, :] = dot(key_faded, value_ref[0, :, cols], ((1,), (0,)))
            out_ref[at, late, :] = dot(query_faded, grad_ref[0, :, cols], ((1,), (0,)))
            out_ref[at, own, :] = jnp.broadcast_to(from_start[:, BLOCK - 1 : BLOCK], (1, DIM))


def scan_kernel(states_ref, rows_ref, out_ref, tails):
    step = pl.program_id(0)
    early, late = slice(0, DIM), slice(DIM, 2 * DIM)

    @pl.when(step == 0)
    def _():
        tails[...] = jnp.zeros_like(tails)

    @pl.when(step < PER)
    def _():
        own = pl.ds(step, 1)
        prior = jnp.zeros((DIM, DIM), F32)
        pushes = []
        for n in range(GROUPS):
            out_ref[n, early, :] = prior
            pushes.append(rounded_sum(prior, states_ref[n, late, :]))
            prior = states_ref[n, early, :] + rows_ref[n, own, :] * prior
        later = jnp.zeros((DIM, DIM), F32)
        tail = jnp.zeros((1, DIM), F32)
        for n in reversed(range(GROUPS)):
            out_ref[n, late, :] = later
            tails[n, own, :] = tail
            tail = tail + pushes[n] - rounded_sum(later, states_ref[n, early, :])
            later = states_ref[n, late, :] + rows_ref[n, own, :] * later

    @pl.when(step == PER)
    def _():
        out_ref[:, :8, :] = tails[...]


def local_kernel(
    query_ref, key_ref, value_ref, grad_ref, running_ref,
    ql_ref, kl_ref, vl_ref, qt_ref, kt_ref, push_ref,
):
    first = lax.broadcasted_iota(jnp.int32, (BLOCK, BLOCK), 0)
    second = lax.broadcasted_iota(jnp.int32, (BLOCK, BLOCK), 1)
    causal = first >= second
    for j in range(LOCAL_HEADS):
        cols = slice(j * DIM, (j + 1) * DIM)
        head = pl.ds(pl.program_id(0) * LOCAL_HEADS + j, 1)
        row = running_ref[head, :]
        column = jnp.concatenate([as_column(row)] * (BLOCK // DIM), axis=1)
        decay = jnp.exp(jnp.where(causal, column - row, -1e30)) * SCALE
        query, key = query_ref[0, :, cols], key_ref[0, :, cols]
        value, grad = value_ref[0, :, cols], grad_ref[0, :, cols]
        weighted = (dot(query, key, ((1,), (1,))) * decay).astype(BF16)
        mixing = (dot(grad, value, ((1,), (1,))) * decay).astype(BF16)
        query_local = dot(mixing, key, ((1,), (0,)))
        key_local = dot(mixing, query, ((0,), (0,)))
        qt_ref[cols, :] = query.T
        kt_ref[cols, :] = key.T
        ql_ref[:, cols] = query_local.astype(BF16)
        kl_ref[:, cols] = key_local.astype(BF16)
        vl_ref[:, cols] = dot(weighted, grad, ((0,), (0,))).astype(BF16)
        push_ref[head, :] = row_sums(
            query.astype(F32) * query_local - key.astype(F32) * key_local
        )


def term_kernel(
    query_ref, key_ref, value_ref, grad_ref, decay_ref, carried_ref, local_ref, slope_ref,
    input_ref, out_ref, push,
):
    step = pl.program_id(0)

    @pl.when(step < TERM_STEPS)
    def _():
        last = lax.broadcasted_iota(jnp.int32, (1, BLOCK), 1) == BLOCK - 1
        for j in range(TERM_HEADS):
            head = step * TERM_HEADS + j
            cols = slice(j * DIM, (j + 1) * DIM)
            at, early, late, own = travelling(j)
            prior = carried_ref[at, early, :].astype(BF16)
            later = carried_ref[at, late, :].astype(BF16)
            query_state = dot(prior, grad_ref[0, :, cols], ((1,), (1,)))
            key_state = dot(later, value_ref[0, :, cols], ((1,), (1,)))
            from_query = jnp.sum(
                query_ref[cols, :].astype(F32) * query_state, axis=0, keepdims=True
            ) * (decay_ref[pl.ds(head, 1), :] * SCALE)
            from_key = jnp.sum(
                key_ref[cols, :].astype(F32) * key_state, axis=0, keepdims=True
            ) * (decay_ref[pl.ds(HEADS + head, 1), :] * SCALE)
            tail = jnp.sum(carried_ref[at, own, :], axis=1, keepdims=True)
            push[pl.ds(head, 1), :] = (
                from_query - from_key + local_ref[pl.ds(head, 1), :] + jnp.where(last, tail, 0.0)
            )

    @pl.when(step == TERM_STEPS - 1)
    def _():
        first = lax.broadcasted_iota(jnp.int32, (BLOCK, BLOCK), 0)
        second = lax.broadcasted_iota(jnp.int32, (BLOCK, BLOCK), 1)
        lower = (first >= second).astype(F32)
        gate_grad = jnp.dot(
            push[...], lower, precision=lax.Precision.HIGHEST, preferred_element_type=F32
        )
        push[...] = gate_grad * slope_ref[...]

    @pl.when(step >= TERM_STEPS)
    def _():
        logit_grad = push[...].astype(BF16)
        for i in range(TERM_OWNERS):
            cols = slice(i * BLOCK, (i + 1) * BLOCK)
            out_ref[i] = dot(logit_grad, input_ref[0, :, cols], ((1,), (0,)))


def full_kernel(
    key_ref, value_ref, grad_ref, decay_ref, carried_ref, ql_ref, kl_ref, vl_ref,
    query_out, key_out, value_out,
):
    for j in range(FULL_HEADS):
        cols = slice(j * DIM, (j + 1) * DIM)
        head = pl.program_id(0) * FULL_HEADS + j
        from_start = as_column(decay_ref[pl.ds(head, 1), :] * SCALE)
        to_end = as_column(decay_ref[pl.ds(HEADS + head, 1), :] * SCALE)
        at, early, late, _ = travelling(j)
        prior = carried_ref[at, early, :].astype(BF16)
        later = carried_ref[at, late, :].astype(BF16)
        query_state = from_start * dot(grad_ref[0, :, cols], prior, ((1,), (1,)))
        key_state = to_end * dot(value_ref[0, :, cols], later, ((1,), (1,)))
        value_state = to_end * dot(key_ref[0, :, cols], later, ((1,), (0,)))
        query_out[0, :, cols] = (ql_ref[:, cols].astype(F32) + query_state).astype(BF16)
        key_out[0, :, cols] = (kl_ref[:, cols].astype(F32) + key_state).astype(BF16)
        value_out[0, :, cols] = (vl_ref[:, cols].astype(F32) + value_state).astype(BF16)


def same(i):
    return i


def heads_block(heads, group=same):
    return pl.BlockSpec((1, BLOCK, heads * DIM), lambda i: (0, 0, group(i)))


def carried_block(heads, group=same):
    return pl.BlockSpec((heads // PER, ROWS, DIM), lambda i: (group(i), 0, 0))


def flat_block(heads, group=same):
    return pl.BlockSpec((BLOCK, heads * DIM), lambda i: (0, group(i)))


def turned_block(heads, group=same):
    return pl.BlockSpec((heads * DIM, BLOCK), lambda i: (group(i), 0))


def whole_block(*dims):
    return pl.BlockSpec(dims, lambda i: (0,) * len(dims))


shape = jax.ShapeDtypeStruct
ROW_TABLE = (HEADS, BLOCK)
DECAY_TABLE = (2 * HEADS, BLOCK)
TRAVELLING = (GROUPS, ROWS, DIM)
FLAT = (BLOCK, HEADS * DIM)
OUT = (1, BLOCK, HEADS * DIM)


def states_of(layer_input, gate_weight, decay_rate, *heads):
    def feature(i):
        return jnp.minimum(i, GATE_STEPS - 1)

    def behind(i):
        return jnp.maximum(i - GATE_STEPS, 0)

    return pl.pallas_call(
        state_kernel,
        grid=(GATE_STEPS + HEADS // STATE_HEADS,),
        in_specs=[
            pl.BlockSpec((1, BLOCK, GATE_STEP), lambda i: (0, 0, feature(i))),
            pl.BlockSpec((HEADS, GATE_STEP), lambda i: (0, feature(i))),
            whole_block(1, HEADS, BLOCK),
        ]
        + [heads_block(STATE_HEADS, behind)] * 4,
        out_specs=[whole_block(*ROW_TABLE)] * 2
        + [whole_block(*DECAY_TABLE), carried_block(STATE_HEADS, behind)],
        out_shape=[shape(ROW_TABLE, F32)] * 2
        + [shape(DECAY_TABLE, F32), shape(TRAVELLING, F32)],
        scratch_shapes=[pltpu.VMEM(ROW_TABLE, F32)],
        compiler_params=limit(60),
        name="states",
    )(layer_input, gate_weight.T, decay_rate, *heads)


def locals_of(running, *heads):
    return pl.pallas_call(
        local_kernel,
        grid=(HEADS // LOCAL_HEADS,),
        in_specs=[heads_block(LOCAL_HEADS)] * 4 + [whole_block(*ROW_TABLE)],
        out_specs=[flat_block(LOCAL_HEADS)] * 3
        + [turned_block(LOCAL_HEADS)] * 2
        + [whole_block(*ROW_TABLE)],
        out_shape=[pltpu.HBM(FLAT, BF16)] * 3
        + [pltpu.HBM((HEADS * DIM, BLOCK), BF16)] * 2
        + [shape(ROW_TABLE, F32)],
        compiler_params=limit(48),
        name="locals",
    )(*in_hbm(*heads), running)


def scanned(states):
    def ahead(i):
        return jnp.minimum(i, PER - 1)

    return pl.pallas_call(
        scan_kernel,
        grid=(PER + 1,),
        in_specs=[
            pl.BlockSpec((GROUPS, 2 * DIM, DIM), lambda i: (0, ahead(i), 0)),
            pl.BlockSpec((GROUPS, 8, DIM), lambda i: (0, 2 * DIM * PER // 8, 0)),
        ],
        out_specs=pl.BlockSpec((GROUPS, 2 * DIM, DIM), lambda i: (0, i, 0)),
        out_shape=pltpu.HBM(TRAVELLING, F32),
        scratch_shapes=[pltpu.VMEM((GROUPS, 8, DIM), F32)],
        compiler_params=limit(32),
        name="scan",
    )(in_vmem(states), in_vmem(states))


def exchanged(array, axis="seq"):
    return lax.all_to_all(array, axis, 0, 0, tiled=True)


def in_hbm(*arrays):
    return [pltpu.with_memory_space_constraint(array, pltpu.HBM) for array in arrays]


def in_vmem(array):
    return pltpu.with_memory_space_constraint(array, pltpu.VMEM)


def summed_over_dp(part):
    count = lax.axis_size("dp")
    pair = part + lax.ppermute(part, "dp", [(i, i ^ 1) for i in range(count)])
    first, second, third = (
        lax.ppermute(pair, "dp", [(i, (i + 2 * step) % count) for i in range(count)])
        for step in (1, 2, 3)
    )
    return (pair + second) + (first + third)


def terms_of(turned, pair, decay, carried, local_push, slope, layer_input):
    def ahead(i):
        return jnp.minimum(i, TERM_STEPS - 1)

    def beyond(i):
        return jnp.maximum(i - TERM_STEPS, 0)

    return pl.pallas_call(
        term_kernel,
        grid=(TERM_STEPS + GROUPS // TERM_OWNERS,),
        in_specs=[turned_block(TERM_HEADS, ahead)] * 2
        + [heads_block(TERM_HEADS, ahead)] * 2
        + [
            whole_block(*DECAY_TABLE),
            carried_block(TERM_HEADS, ahead),
            whole_block(*ROW_TABLE),
            whole_block(*ROW_TABLE),
            pl.BlockSpec((1, BLOCK, TERM_OWNERS * BLOCK), lambda i: (0, 0, beyond(i))),
        ],
        out_specs=pl.BlockSpec((TERM_OWNERS, HEADS, BLOCK), lambda i: (beyond(i), 0, 0)),
        out_shape=pltpu.HBM((GROUPS, HEADS, BLOCK), F32),
        scratch_shapes=[pltpu.VMEM(ROW_TABLE, F32)],
        compiler_params=limit(48),
        name="terms",
    )(
        *in_hbm(*turned, *pair), decay, in_vmem(carried), local_push, slope, *in_hbm(layer_input)
    )


def full_of(heads, decay, carried, *local_parts):
    return pl.pallas_call(
        full_kernel,
        grid=(HEADS // FULL_HEADS,),
        in_specs=[heads_block(FULL_HEADS)] * 3
        + [whole_block(*DECAY_TABLE), carried_block(FULL_HEADS)]
        + [flat_block(FULL_HEADS)] * 3,
        out_specs=[heads_block(FULL_HEADS)] * 3,
        out_shape=[shape(OUT, BF16)] * 3,
        compiler_params=limit(48),
        name="full",
    )(*in_hbm(*heads), decay, in_vmem(carried), *in_hbm(*local_parts))


def after(array, *others):
    return lax.optimization_barrier((array, *others))[0]


def local(query_heads, key_heads, value_heads, output_grad, layer_input, gate_weight, decay_rate):
    heads = (query_heads, key_heads, value_heads, output_grad)
    running, slope, decay, states = states_of(layer_input, gate_weight, decay_rate, *heads)
    carried = exchanged(scanned(exchanged(states)))
    *local_parts, query_turned, key_turned, local_push = locals_of(running, *heads)
    turned = (query_turned, key_turned)
    terms = exchanged(
        terms_of(turned, heads[2:], decay, carried, local_push, slope, layer_input)
    )
    grads = full_of(heads[1:], decay, carried, *local_parts)
    sums = after(jnp.sum(terms, axis=0), grads[0])
    token_count = BLOCK * lax.axis_size("seq") * lax.axis_size("dp")
    weight_grad = summed_over_dp(sums) / token_count
    return *grads, weight_grad


def solution(mesh):
    heads = P("dp", "seq", None)
    return jax.shard_map(
        local,
        mesh=mesh,
        in_specs=(heads,) * 5 + (P(), P("dp", None, "seq")),
        out_specs=(heads,) * 3 + (P(None, "seq"),),
        check_vma=False,
    )
```

```python
import jax
import jax.numpy as jnp
from jax import lax
from jax.experimental import pallas as pl
from jax.experimental.pallas import tpu as pltpu
from jax.sharding import PartitionSpec as P

F32 = jnp.float32
BF16 = jnp.bfloat16
BLOCK = 384
HEADS = 32
DIM = 128
MODEL = 6144
GROUPS = 16
PER = HEADS // GROUPS
ROWS = 2 * DIM * PER + 8
SCALE = 1.0 / DIM
GATE_STEP = 128
GATE_STEPS = BLOCK // GATE_STEP
STATE_HEADS = 8
LOCAL_HEADS = 2
TERM_HEADS = 8
TERM_STEPS = HEADS // TERM_HEADS
FULL_HEADS = 8
TERM_OWNERS = 8


def limit(mib):
    return pltpu.CompilerParams(vmem_limit_bytes=mib * 1024 * 1024)


def dot(a, b, dims):
    return lax.dot_general(a, b, (dims, ((), ())), preferred_element_type=F32)


def rounded_sum(rounded, other):
    return jnp.sum(rounded.astype(BF16).astype(F32) * other, axis=0, keepdims=True) * SCALE


def as_column(row):
    return jnp.broadcast_to(row, (DIM, BLOCK)).T


def row_sums(rows):
    ones = jnp.ones((8, DIM), BF16)
    high = rows.astype(BF16)
    low = (rows - high.astype(F32)).astype(BF16)
    both = dot(ones, high, ((1,), (1,))) + dot(ones, low, ((1,), (1,)))
    return both[0:1]


def travelling(head):
    base = 2 * DIM * (head % PER)
    own = 2 * DIM * PER + head % PER
    return (
        head // PER,
        slice(base, base + DIM),
        slice(base + DIM, base + 2 * DIM),
        slice(own, own + 1),
    )


def state_kernel(
    input_ref, weight_ref, rate_ref, query_ref, key_ref, value_ref, grad_ref,
    running_ref, slope_ref, decay_ref, out_ref, logits,
):
    step = pl.program_id(0)

    @pl.when(step < GATE_STEPS)
    def _():
        cols = pl.ds(pl.multiple_of(step * GATE_STEP, GATE_STEP), GATE_STEP)
        logits[:, cols] = dot(weight_ref[...], input_ref[0], ((1,), (1,)))

    @pl.when(step == GATE_STEPS - 1)
    def _():
        gate_open = jax.nn.sigmoid(logits[...])
        log_gate = -2.0 * rate_ref[0] * gate_open
        first = lax.broadcasted_iota(jnp.int32, (BLOCK, BLOCK), 0)
        second = lax.broadcasted_iota(jnp.int32, (BLOCK, BLOCK), 1)
        upper = (first <= second).astype(F32)
        running = jnp.dot(
            log_gate, upper, precision=lax.Precision.HIGHEST, preferred_element_type=F32
        )
        running_ref[...] = running
        slope_ref[...] = log_gate * (1.0 - gate_open)
        decay_ref[:HEADS, :] = jnp.exp(running)
        decay_ref[HEADS:, :] = jnp.exp(running[:, BLOCK - 1 : BLOCK] - running)

    @pl.when(step >= GATE_STEPS)
    def _():
        out_ref[:, 2 * DIM * PER :, :] = jnp.zeros((STATE_HEADS // PER, 8, DIM), F32)
        for j in range(STATE_HEADS):
            cols = slice(j * DIM, (j + 1) * DIM)
            head = (step - GATE_STEPS) * STATE_HEADS + j
            from_start = decay_ref[pl.ds(head, 1), :]
            to_end = decay_ref[pl.ds(HEADS + head, 1), :]
            key_faded = (key_ref[0, :, cols].T.astype(F32) * to_end).astype(BF16)
            query_faded = (query_ref[0, :, cols].T.astype(F32) * from_start).astype(BF16)
            at, early, late, own = travelling(j)
            out_ref[at, early, :] = dot(key_faded, value_ref[0, :, cols], ((1,), (0,)))
            out_ref[at, late, :] = dot(query_faded, grad_ref[0, :, cols], ((1,), (0,)))
            out_ref[at, own, :] = jnp.broadcast_to(from_start[:, BLOCK - 1 : BLOCK], (1, DIM))


def scan_kernel(states_ref, rows_ref, out_ref, tails):
    step = pl.program_id(0)
    early, late = slice(0, DIM), slice(DIM, 2 * DIM)

    @pl.when(step == 0)
    def _():
        tails[...] = jnp.zeros_like(tails)

    @pl.when(step < PER)
    def _():
        own = pl.ds(step, 1)
        prior = jnp.zeros((DIM, DIM), F32)
        pushes = []
        for n in range(GROUPS):
            out_ref[n, early, :] = prior
            pushes.append(rounded_sum(prior, states_ref[n, late, :]))
            prior = states_ref[n, early, :] + rows_ref[n, own, :] * prior
        later = jnp.zeros((DIM, DIM), F32)
        tail = jnp.zeros((1, DIM), F32)
        for n in reversed(range(GROUPS)):
            out_ref[n, late, :] = later
            tails[n, own, :] = tail
            tail = tail + pushes[n] - rounded_sum(later, states_ref[n, early, :])
            later = states_ref[n, late, :] + rows_ref[n, own, :] * later

    @pl.when(step == PER)
    def _():
        out_ref[:, :8, :] = tails[...]


def local_kernel(
    query_ref, key_ref, value_ref, grad_ref, running_ref,
    ql_ref, kl_ref, vl_ref, qt_ref, kt_ref, push_ref,
):
    first = lax.broadcasted_iota(jnp.int32, (BLOCK, BLOCK), 0)
    second = lax.broadcasted_iota(jnp.int32, (BLOCK, BLOCK), 1)
    causal = first >= second
    for j in range(LOCAL_HEADS):
        cols = slice(j * DIM, (j + 1) * DIM)
        head = pl.ds(pl.program_id(0) * LOCAL_HEADS + j, 1)
        row = running_ref[head, :]
        column = jnp.concatenate([as_column(row)] * (BLOCK // DIM), axis=1)
        decay = jnp.exp(jnp.where(causal, column - row, -1e30)) * SCALE
        query, key = query_ref[0, :, cols], key_ref[0, :, cols]
        value, grad = value_ref[0, :, cols], grad_ref[0, :, cols]
        weighted = (dot(query, key, ((1,), (1,))) * decay).astype(BF16)
        mixing = (dot(grad, value, ((1,), (1,))) * decay).astype(BF16)
        query_local = dot(mixing, key, ((1,), (0,)))
        key_local = dot(mixing, query, ((0,), (0,)))
        qt_ref[cols, :] = query.T
        kt_ref[cols, :] = key.T
        ql_ref[:, cols] = query_local.astype(BF16)
        kl_ref[:, cols] = key_local.astype(BF16)
        vl_ref[:, cols] = dot(weighted, grad, ((0,), (0,))).astype(BF16)
        push_ref[head, :] = row_sums(
            query.astype(F32) * query_local - key.astype(F32) * key_local
        )


def term_kernel(
    query_ref, key_ref, value_ref, grad_ref, decay_ref, carried_ref, local_ref, slope_ref,
    input_ref, out_ref, push,
):
    step = pl.program_id(0)

    @pl.when(step < TERM_STEPS)
    def _():
        last = lax.broadcasted_iota(jnp.int32, (1, BLOCK), 1) == BLOCK - 1
        for j in range(TERM_HEADS):
            head = step * TERM_HEADS + j
            cols = slice(j * DIM, (j + 1) * DIM)
            at, early, late, own = travelling(j)
            prior = carried_ref[at, early, :].astype(BF16)
            later = carried_ref[at, late, :].astype(BF16)
            query_state = dot(prior, grad_ref[0, :, cols], ((1,), (1,)))
            key_state = dot(later, value_ref[0, :, cols], ((1,), (1,)))
            from_query = jnp.sum(
                query_ref[cols, :].astype(F32) * query_state, axis=0, keepdims=True
            ) * (decay_ref[pl.ds(head, 1), :] * SCALE)
            from_key = jnp.sum(
                key_ref[cols, :].astype(F32) * key_state, axis=0, keepdims=True
            ) * (decay_ref[pl.ds(HEADS + head, 1), :] * SCALE)
            tail = jnp.sum(carried_ref[at, own, :], axis=1, keepdims=True)
            push[pl.ds(head, 1), :] = (
                from_query - from_key + local_ref[pl.ds(head, 1), :] + jnp.where(last, tail, 0.0)
            )

    @pl.when(step == TERM_STEPS - 1)
    def _():
        first = lax.broadcasted_iota(jnp.int32, (BLOCK, BLOCK), 0)
        second = lax.broadcasted_iota(jnp.int32, (BLOCK, BLOCK), 1)
        lower = (first >= second).astype(F32)
        gate_grad = jnp.dot(
            push[...], lower, precision=lax.Precision.HIGHEST, preferred_element_type=F32
        )
        push[...] = gate_grad * slope_ref[...]

    @pl.when(step >= TERM_STEPS)
    def _():
        logit_grad = push[...].astype(BF16)
        for i in range(TERM_OWNERS):
            cols = slice(i * BLOCK, (i + 1) * BLOCK)
            out_ref[i] = dot(logit_grad, input_ref[0, :, cols], ((1,), (0,)))


def full_kernel(
    key_ref, value_ref, grad_ref, decay_ref, carried_ref, ql_ref, kl_ref, vl_ref,
    query_out, key_out, value_out,
):
    for j in range(FULL_HEADS):
        cols = slice(j * DIM, (j + 1) * DIM)
        head = pl.program_id(0) * FULL_HEADS + j
        from_start = as_column(decay_ref[pl.ds(head, 1), :] * SCALE)
        to_end = as_column(decay_ref[pl.ds(HEADS + head, 1), :] * SCALE)
        at, early, late, _ = travelling(j)
        prior = carried_ref[at, early, :].astype(BF16)
        later = carried_ref[at, late, :].astype(BF16)
        query_state = from_start * dot(grad_ref[0, :, cols], prior, ((1,), (1,)))
        key_state = to_end * dot(value_ref[0, :, cols], later, ((1,), (1,)))
        value_state = to_end * dot(key_ref[0, :, cols], later, ((1,), (0,)))
        query_out[0, :, cols] = (ql_ref[:, cols].astype(F32) + query_state).astype(BF16)
        key_out[0, :, cols] = (kl_ref[:, cols].astype(F32) + key_state).astype(BF16)
        value_out[0, :, cols] = (vl_ref[:, cols].astype(F32) + value_state).astype(BF16)


def same(i):
    return i


def heads_block(heads, group=same):
    return pl.BlockSpec((1, BLOCK, heads * DIM), lambda i: (0, 0, group(i)))


def carried_block(heads, group=same):
    return pl.BlockSpec((heads // PER, ROWS, DIM), lambda i: (group(i), 0, 0))


def flat_block(heads, group=same):
    return pl.BlockSpec((BLOCK, heads * DIM), lambda i: (0, group(i)))


def turned_block(heads, group=same):
    return pl.BlockSpec((heads * DIM, BLOCK), lambda i: (group(i), 0))


def whole_block(*dims):
    return pl.BlockSpec(dims, lambda i: (0,) * len(dims))


shape = jax.ShapeDtypeStruct
ROW_TABLE = (HEADS, BLOCK)
DECAY_TABLE = (2 * HEADS, BLOCK)
TRAVELLING = (GROUPS, ROWS, DIM)
FLAT = (BLOCK, HEADS * DIM)
OUT = (1, BLOCK, HEADS * DIM)


def states_of(layer_input, gate_weight, decay_rate, *heads):
    def position(i):
        return jnp.minimum(i, GATE_STEPS - 1)

    def behind(i):
        return jnp.maximum(i - GATE_STEPS, 0)

    return pl.pallas_call(
        state_kernel,
        grid=(GATE_STEPS + HEADS // STATE_HEADS,),
        in_specs=[
            pl.BlockSpec((1, GATE_STEP, MODEL), lambda i: (0, position(i), 0)),
            whole_block(HEADS, MODEL),
            whole_block(1, HEADS, BLOCK),
        ]
        + [heads_block(STATE_HEADS, behind)] * 4,
        out_specs=[whole_block(*ROW_TABLE)] * 2
        + [whole_block(*DECAY_TABLE), carried_block(STATE_HEADS, behind)],
        out_shape=[shape(ROW_TABLE, F32)] * 2
        + [shape(DECAY_TABLE, F32), shape(TRAVELLING, F32)],
        scratch_shapes=[pltpu.VMEM(ROW_TABLE, F32)],
        compiler_params=limit(60),
        name="states",
    )(layer_input, gate_weight.T, decay_rate, *heads)


def locals_of(running, *heads):
    return pl.pallas_call(
        local_kernel,
        grid=(HEADS // LOCAL_HEADS,),
        in_specs=[heads_block(LOCAL_HEADS)] * 4 + [whole_block(*ROW_TABLE)],
        out_specs=[flat_block(LOCAL_HEADS)] * 3
        + [turned_block(LOCAL_HEADS)] * 2
        + [whole_block(*ROW_TABLE)],
        out_shape=[pltpu.HBM(FLAT, BF16)] * 3
        + [pltpu.HBM((HEADS * DIM, BLOCK), BF16)] * 2
        + [shape(ROW_TABLE, F32)],
        compiler_params=limit(30),
        name="locals",
    )(*in_hbm(*heads), running)


def scanned(states):
    def ahead(i):
        return jnp.minimum(i, PER - 1)

    return pl.pallas_call(
        scan_kernel,
        grid=(PER + 1,),
        in_specs=[
            pl.BlockSpec((GROUPS, 2 * DIM, DIM), lambda i: (0, ahead(i), 0)),
            pl.BlockSpec((GROUPS, 8, DIM), lambda i: (0, 2 * DIM * PER // 8, 0)),
        ],
        out_specs=pl.BlockSpec((GROUPS, 2 * DIM, DIM), lambda i: (0, i, 0)),
        out_shape=pltpu.HBM(TRAVELLING, F32),
        scratch_shapes=[pltpu.VMEM((GROUPS, 8, DIM), F32)],
        compiler_params=limit(32),
        name="scan",
    )(in_vmem(states), in_vmem(states))


def exchanged(array, axis="seq"):
    return lax.all_to_all(array, axis, 0, 0, tiled=True)


def in_hbm(*arrays):
    return [pltpu.with_memory_space_constraint(array, pltpu.HBM) for array in arrays]


def in_vmem(array):
    return pltpu.with_memory_space_constraint(array, pltpu.VMEM)


def summed_over_dp(part):
    count = lax.axis_size("dp")
    pair = part + lax.ppermute(part, "dp", [(i, i ^ 1) for i in range(count)])
    first, second, third = (
        lax.ppermute(pair, "dp", [(i, (i + 2 * step) % count) for i in range(count)])
        for step in (1, 2, 3)
    )
    return (pair + second) + (first + third)


def terms_of(turned, pair, decay, carried, local_push, slope, layer_input):
    def ahead(i):
        return jnp.minimum(i, TERM_STEPS - 1)

    def beyond(i):
        return jnp.maximum(i - TERM_STEPS, 0)

    return pl.pallas_call(
        term_kernel,
        grid=(TERM_STEPS + GROUPS // TERM_OWNERS,),
        in_specs=[turned_block(TERM_HEADS, ahead)] * 2
        + [heads_block(TERM_HEADS, ahead)] * 2
        + [
            whole_block(*DECAY_TABLE),
            carried_block(TERM_HEADS, ahead),
            whole_block(*ROW_TABLE),
            whole_block(*ROW_TABLE),
            pl.BlockSpec((1, BLOCK, TERM_OWNERS * BLOCK), lambda i: (0, 0, beyond(i))),
        ],
        out_specs=pl.BlockSpec((TERM_OWNERS, HEADS, BLOCK), lambda i: (beyond(i), 0, 0)),
        out_shape=pltpu.HBM((GROUPS, HEADS, BLOCK), F32),
        scratch_shapes=[pltpu.VMEM(ROW_TABLE, F32)],
        compiler_params=limit(30),
        name="terms",
    )(
        *in_hbm(*turned, *pair), decay, in_vmem(carried), local_push, slope, *in_hbm(layer_input)
    )


def full_of(heads, decay, carried, *local_parts):
    return pl.pallas_call(
        full_kernel,
        grid=(HEADS // FULL_HEADS,),
        in_specs=[heads_block(FULL_HEADS)] * 3
        + [whole_block(*DECAY_TABLE), carried_block(FULL_HEADS)]
        + [flat_block(FULL_HEADS)] * 3,
        out_specs=[heads_block(FULL_HEADS)] * 3,
        out_shape=[shape(OUT, BF16)] * 3,
        compiler_params=limit(30),
        name="full",
    )(*in_hbm(*heads), decay, in_vmem(carried), *in_hbm(*local_parts))


def after(array, *others):
    return lax.optimization_barrier((array, *others))[0]


def local(query_heads, key_heads, value_heads, output_grad, layer_input, gate_weight, decay_rate):
    heads = (query_heads, key_heads, value_heads, output_grad)
    running, slope, decay, states = states_of(layer_input, gate_weight, decay_rate, *heads)
    carried = exchanged(scanned(exchanged(states)))
    *local_parts, query_turned, key_turned, local_push = locals_of(running, *heads)
    turned = (query_turned, key_turned)
    terms = exchanged(
        terms_of(turned, heads[2:], decay, carried, local_push, slope, layer_input)
    )
    grads = full_of(heads[1:], decay, carried, *local_parts)
    sums = after(jnp.sum(terms, axis=0), grads[0])
    token_count = BLOCK * lax.axis_size("seq") * lax.axis_size("dp")
    weight_grad = summed_over_dp(sums) / token_count
    return *grads, weight_grad


def solution(mesh):
    heads = P("dp", "seq", None)
    return jax.shard_map(
        local,
        mesh=mesh,
        in_specs=(heads,) * 5 + (P(), P("dp", None, "seq")),
        out_specs=(heads,) * 3 + (P(None, "seq"),),
        check_vma=False,
    )
```

```python
import jax
import jax.numpy as jnp
from jax import lax
from jax.experimental import pallas as pl
from jax.experimental.pallas import tpu as pltpu
from jax.sharding import PartitionSpec as P

F32 = jnp.float32
BF16 = jnp.bfloat16
BLOCK = 384
HEADS = 32
DIM = 128
MODEL = 6144
GROUPS = 16
PER = HEADS // GROUPS
ROWS = 2 * DIM * PER + 8
SCALE = 1.0 / DIM
GATE_STEP = 3072
GATE_STEPS = MODEL // GATE_STEP
STATE_HEADS = 8
LOCAL_HEADS = 2
TERM_HEADS = 16
TERM_STEPS = HEADS // TERM_HEADS
FULL_HEADS = 8
TERM_OWNERS = 8


def limit(mib):
    return pltpu.CompilerParams(vmem_limit_bytes=mib * 1024 * 1024)


def dot(a, b, dims):
    return lax.dot_general(a, b, (dims, ((), ())), preferred_element_type=F32)


def rounded_sum(rounded, other):
    return jnp.sum(rounded.astype(BF16).astype(F32) * other, axis=0, keepdims=True) * SCALE


def as_column(row):
    return jnp.broadcast_to(row, (DIM, BLOCK)).T


def row_sums(rows):
    ones = jnp.ones((8, DIM), BF16)
    high = rows.astype(BF16)
    low = (rows - high.astype(F32)).astype(BF16)
    both = dot(ones, high, ((1,), (1,))) + dot(ones, low, ((1,), (1,)))
    return both[0:1]


def travelling(head):
    base = 2 * DIM * (head % PER)
    own = 2 * DIM * PER + head % PER
    return (
        head // PER,
        slice(base, base + DIM),
        slice(base + DIM, base + 2 * DIM),
        slice(own, own + 1),
    )


def state_kernel(
    input_ref, weight_ref, rate_ref, query_ref, key_ref, value_ref, grad_ref,
    running_ref, slope_ref, decay_ref, out_ref, logits,
):
    step = pl.program_id(0)

    @pl.when(step == 0)
    def _():
        logits[...] = dot(weight_ref[...], input_ref[0], ((1,), (1,)))

    @pl.when((step > 0) & (step < GATE_STEPS))
    def _():
        logits[...] += dot(weight_ref[...], input_ref[0], ((1,), (1,)))

    @pl.when(step == GATE_STEPS - 1)
    def _():
        gate_open = jax.nn.sigmoid(logits[...])
        log_gate = -2.0 * rate_ref[0] * gate_open
        first = lax.broadcasted_iota(jnp.int32, (BLOCK, BLOCK), 0)
        second = lax.broadcasted_iota(jnp.int32, (BLOCK, BLOCK), 1)
        upper = (first <= second).astype(F32)
        running = jnp.dot(
            log_gate, upper, precision=lax.Precision.HIGHEST, preferred_element_type=F32
        )
        running_ref[...] = running
        slope_ref[...] = log_gate * (1.0 - gate_open)
        decay_ref[:HEADS, :] = jnp.exp(running)
        decay_ref[HEADS:, :] = jnp.exp(running[:, BLOCK - 1 : BLOCK] - running)

    @pl.when(step >= GATE_STEPS)
    def _():
        out_ref[:, 2 * DIM * PER :, :] = jnp.zeros((STATE_HEADS // PER, 8, DIM), F32)
        for j in range(STATE_HEADS):
            cols = slice(j * DIM, (j + 1) * DIM)
            head = (step - GATE_STEPS) * STATE_HEADS + j
            from_start = decay_ref[pl.ds(head, 1), :]
            to_end = decay_ref[pl.ds(HEADS + head, 1), :]
            key_faded = (key_ref[0, :, cols].T.astype(F32) * to_end).astype(BF16)
            query_faded = (query_ref[0, :, cols].T.astype(F32) * from_start).astype(BF16)
            at, early, late, own = travelling(j)
            out_ref[at, early, :] = dot(key_faded, value_ref[0, :, cols], ((1,), (0,)))
            out_ref[at, late, :] = dot(query_faded, grad_ref[0, :, cols], ((1,), (0,)))
            out_ref[at, own, :] = jnp.broadcast_to(from_start[:, BLOCK - 1 : BLOCK], (1, DIM))


def scan_kernel(states_ref, rows_ref, out_ref, tails):
    step = pl.program_id(0)
    early, late = slice(0, DIM), slice(DIM, 2 * DIM)

    @pl.when(step == 0)
    def _():
        tails[...] = jnp.zeros_like(tails)

    @pl.when(step < PER)
    def _():
        own = pl.ds(step, 1)
        prior = jnp.zeros((DIM, DIM), F32)
        pushes = []
        for n in range(GROUPS):
            out_ref[n, early, :] = prior
            pushes.append(rounded_sum(prior, states_ref[n, late, :]))
            prior = states_ref[n, early, :] + rows_ref[n, own, :] * prior
        later = jnp.zeros((DIM, DIM), F32)
        tail = jnp.zeros((1, DIM), F32)
        for n in reversed(range(GROUPS)):
            out_ref[n, late, :] = later
            tails[n, own, :] = tail
            tail = tail + pushes[n] - rounded_sum(later, states_ref[n, early, :])
            later = states_ref[n, late, :] + rows_ref[n, own, :] * later

    @pl.when(step == PER)
    def _():
        out_ref[:, :8, :] = tails[...]


def local_kernel(
    query_ref, key_ref, value_ref, grad_ref, running_ref,
    ql_ref, kl_ref, vl_ref, qt_ref, kt_ref, push_ref,
):
    first = lax.broadcasted_iota(jnp.int32, (BLOCK, BLOCK), 0)
    second = lax.broadcasted_iota(jnp.int32, (BLOCK, BLOCK), 1)
    causal = first >= second
    for j in range(LOCAL_HEADS):
        cols = slice(j * DIM, (j + 1) * DIM)
        head = pl.ds(pl.program_id(0) * LOCAL_HEADS + j, 1)
        row = running_ref[head, :]
        column = jnp.concatenate([as_column(row)] * (BLOCK // DIM), axis=1)
        decay = jnp.exp(jnp.where(causal, column - row, -1e30)) * SCALE
        query, key = query_ref[0, :, cols], key_ref[0, :, cols]
        value, grad = value_ref[0, :, cols], grad_ref[0, :, cols]
        weighted = (dot(query, key, ((1,), (1,))) * decay).astype(BF16)
        mixing = (dot(grad, value, ((1,), (1,))) * decay).astype(BF16)
        query_local = dot(mixing, key, ((1,), (0,)))
        key_local = dot(mixing, query, ((0,), (0,)))
        qt_ref[cols, :] = query.T
        kt_ref[cols, :] = key.T
        ql_ref[:, cols] = query_local.astype(BF16)
        kl_ref[:, cols] = key_local.astype(BF16)
        vl_ref[:, cols] = dot(weighted, grad, ((0,), (0,))).astype(BF16)
        push_ref[head, :] = row_sums(
            query.astype(F32) * query_local - key.astype(F32) * key_local
        )


def term_kernel(
    query_ref, key_ref, value_ref, grad_ref, decay_ref, carried_ref, local_ref, slope_ref,
    input_ref, out_ref, push,
):
    step = pl.program_id(0)

    @pl.when(step < TERM_STEPS)
    def _():
        last = lax.broadcasted_iota(jnp.int32, (1, BLOCK), 1) == BLOCK - 1
        for j in range(TERM_HEADS):
            head = step * TERM_HEADS + j
            cols = slice(j * DIM, (j + 1) * DIM)
            at, early, late, own = travelling(j)
            prior = carried_ref[at, early, :].astype(BF16)
            later = carried_ref[at, late, :].astype(BF16)
            query_state = dot(prior, grad_ref[0, :, cols], ((1,), (1,)))
            key_state = dot(later, value_ref[0, :, cols], ((1,), (1,)))
            from_query = jnp.sum(
                query_ref[cols, :].astype(F32) * query_state, axis=0, keepdims=True
            ) * (decay_ref[pl.ds(head, 1), :] * SCALE)
            from_key = jnp.sum(
                key_ref[cols, :].astype(F32) * key_state, axis=0, keepdims=True
            ) * (decay_ref[pl.ds(HEADS + head, 1), :] * SCALE)
            tail = jnp.sum(carried_ref[at, own, :], axis=1, keepdims=True)
            push[pl.ds(head, 1), :] = (
                from_query - from_key + local_ref[pl.ds(head, 1), :] + jnp.where(last, tail, 0.0)
            )

    @pl.when(step == TERM_STEPS - 1)
    def _():
        first = lax.broadcasted_iota(jnp.int32, (BLOCK, BLOCK), 0)
        second = lax.broadcasted_iota(jnp.int32, (BLOCK, BLOCK), 1)
        lower = (first >= second).astype(F32)
        gate_grad = jnp.dot(
            push[...], lower, precision=lax.Precision.HIGHEST, preferred_element_type=F32
        )
        push[...] = gate_grad * slope_ref[...]

    @pl.when(step >= TERM_STEPS)
    def _():
        logit_grad = push[...].astype(BF16)
        for i in range(TERM_OWNERS):
            cols = slice(i * BLOCK, (i + 1) * BLOCK)
            out_ref[i] = dot(logit_grad, input_ref[0, :, cols], ((1,), (0,)))


def full_kernel(
    key_ref, value_ref, grad_ref, decay_ref, carried_ref, ql_ref, kl_ref, vl_ref,
    query_out, key_out, value_out,
):
    for j in range(FULL_HEADS):
        cols = slice(j * DIM, (j + 1) * DIM)
        head = pl.program_id(0) * FULL_HEADS + j
        from_start = as_column(decay_ref[pl.ds(head, 1), :] * SCALE)
        to_end = as_column(decay_ref[pl.ds(HEADS + head, 1), :] * SCALE)
        at, early, late, _ = travelling(j)
        prior = carried_ref[at, early, :].astype(BF16)
        later = carried_ref[at, late, :].astype(BF16)
        query_state = from_start * dot(grad_ref[0, :, cols], prior, ((1,), (1,)))
        key_state = to_end * dot(value_ref[0, :, cols], later, ((1,), (1,)))
        value_state = to_end * dot(key_ref[0, :, cols], later, ((1,), (0,)))
        query_out[0, :, cols] = (ql_ref[:, cols].astype(F32) + query_state).astype(BF16)
        key_out[0, :, cols] = (kl_ref[:, cols].astype(F32) + key_state).astype(BF16)
        value_out[0, :, cols] = (vl_ref[:, cols].astype(F32) + value_state).astype(BF16)


def same(i):
    return i


def heads_block(heads, group=same):
    return pl.BlockSpec((1, BLOCK, heads * DIM), lambda i: (0, 0, group(i)))


def carried_block(heads, group=same):
    return pl.BlockSpec((heads // PER, ROWS, DIM), lambda i: (group(i), 0, 0))


def flat_block(heads, group=same):
    return pl.BlockSpec((BLOCK, heads * DIM), lambda i: (0, group(i)))


def turned_block(heads, group=same):
    return pl.BlockSpec((heads * DIM, BLOCK), lambda i: (group(i), 0))


def whole_block(*dims):
    return pl.BlockSpec(dims, lambda i: (0,) * len(dims))


shape = jax.ShapeDtypeStruct
ROW_TABLE = (HEADS, BLOCK)
DECAY_TABLE = (2 * HEADS, BLOCK)
TRAVELLING = (GROUPS, ROWS, DIM)
FLAT = (BLOCK, HEADS * DIM)
OUT = (1, BLOCK, HEADS * DIM)


def states_of(layer_input, gate_weight, decay_rate, *heads):
    def feature(i):
        return jnp.minimum(i, GATE_STEPS - 1)

    def behind(i):
        return jnp.maximum(i - GATE_STEPS, 0)

    return pl.pallas_call(
        state_kernel,
        grid=(GATE_STEPS + HEADS // STATE_HEADS,),
        in_specs=[
            pl.BlockSpec((1, BLOCK, GATE_STEP), lambda i: (0, 0, feature(i))),
            pl.BlockSpec((HEADS, GATE_STEP), lambda i: (0, feature(i))),
            whole_block(1, HEADS, BLOCK),
        ]
        + [heads_block(STATE_HEADS, behind)] * 4,
        out_specs=[whole_block(*ROW_TABLE)] * 2
        + [whole_block(*DECAY_TABLE), carried_block(STATE_HEADS, behind)],
        out_shape=[shape(ROW_TABLE, F32)] * 2
        + [shape(DECAY_TABLE, F32), shape(TRAVELLING, F32)],
        scratch_shapes=[pltpu.VMEM(ROW_TABLE, F32)],
        compiler_params=limit(60),
        name="states",
    )(layer_input, gate_weight.T, decay_rate, *heads)


def locals_of(running, *heads):
    return pl.pallas_call(
        local_kernel,
        grid=(HEADS // LOCAL_HEADS,),
        in_specs=[heads_block(LOCAL_HEADS)] * 4 + [whole_block(*ROW_TABLE)],
        out_specs=[flat_block(LOCAL_HEADS)] * 3
        + [turned_block(LOCAL_HEADS)] * 2
        + [whole_block(*ROW_TABLE)],
        out_shape=[pltpu.HBM(FLAT, BF16)] * 3
        + [pltpu.HBM((HEADS * DIM, BLOCK), BF16)] * 2
        + [shape(ROW_TABLE, F32)],
        compiler_params=limit(48),
        name="locals",
    )(*in_hbm(*heads), running)


def scanned(states):
    def ahead(i):
        return jnp.minimum(i, PER - 1)

    return pl.pallas_call(
        scan_kernel,
        grid=(PER + 1,),
        in_specs=[
            pl.BlockSpec((GROUPS, 2 * DIM, DIM), lambda i: (0, ahead(i), 0)),
            pl.BlockSpec((GROUPS, 8, DIM), lambda i: (0, 2 * DIM * PER // 8, 0)),
        ],
        out_specs=pl.BlockSpec((GROUPS, 2 * DIM, DIM), lambda i: (0, i, 0)),
        out_shape=pltpu.HBM(TRAVELLING, F32),
        scratch_shapes=[pltpu.VMEM((GROUPS, 8, DIM), F32)],
        compiler_params=limit(32),
        name="scan",
    )(in_vmem(states), in_vmem(states))


def exchanged(array, axis="seq"):
    return lax.all_to_all(array, axis, 0, 0, tiled=True)


def in_hbm(*arrays):
    return [pltpu.with_memory_space_constraint(array, pltpu.HBM) for array in arrays]


def in_vmem(array):
    return pltpu.with_memory_space_constraint(array, pltpu.VMEM)


def summed_over_dp(part):
    count = lax.axis_size("dp")
    pair = part + lax.ppermute(part, "dp", [(i, i ^ 1) for i in range(count)])
    first, second, third = (
        lax.ppermute(pair, "dp", [(i, (i + 2 * step) % count) for i in range(count)])
        for step in (1, 2, 3)
    )
    return (pair + second) + (first + third)


def terms_of(turned, pair, decay, carried, local_push, slope, layer_input):
    def ahead(i):
        return jnp.minimum(i, TERM_STEPS - 1)

    def beyond(i):
        return jnp.maximum(i - TERM_STEPS, 0)

    return pl.pallas_call(
        term_kernel,
        grid=(TERM_STEPS + GROUPS // TERM_OWNERS,),
        in_specs=[turned_block(TERM_HEADS, ahead)] * 2
        + [heads_block(TERM_HEADS, ahead)] * 2
        + [
            whole_block(*DECAY_TABLE),
            carried_block(TERM_HEADS, ahead),
            whole_block(*ROW_TABLE),
            whole_block(*ROW_TABLE),
            pl.BlockSpec((1, BLOCK, TERM_OWNERS * BLOCK), lambda i: (0, 0, beyond(i))),
        ],
        out_specs=pl.BlockSpec((TERM_OWNERS, HEADS, BLOCK), lambda i: (beyond(i), 0, 0)),
        out_shape=pltpu.HBM((GROUPS, HEADS, BLOCK), F32),
        scratch_shapes=[pltpu.VMEM(ROW_TABLE, F32)],
        compiler_params=limit(48),
        name="terms",
    )(
        *in_hbm(*turned, *pair), decay, in_vmem(carried), local_push, slope, *in_hbm(layer_input)
    )


def full_of(heads, decay, carried, *local_parts):
    return pl.pallas_call(
        full_kernel,
        grid=(HEADS // FULL_HEADS,),
        in_specs=[heads_block(FULL_HEADS)] * 3
        + [whole_block(*DECAY_TABLE), carried_block(FULL_HEADS)]
        + [flat_block(FULL_HEADS)] * 3,
        out_specs=[heads_block(FULL_HEADS)] * 3,
        out_shape=[shape(OUT, BF16)] * 3,
        compiler_params=limit(48),
        name="full",
    )(*in_hbm(*heads), decay, in_vmem(carried), *in_hbm(*local_parts))


def after(array, *others):
    return lax.optimization_barrier((array, *others))[0]


def local(query_heads, key_heads, value_heads, output_grad, layer_input, gate_weight, decay_rate):
    heads = (query_heads, key_heads, value_heads, output_grad)
    running, slope, decay, states = states_of(layer_input, gate_weight, decay_rate, *heads)
    carried = exchanged(scanned(exchanged(states)))
    *local_parts, query_turned, key_turned, local_push = locals_of(running, *heads)
    turned = (query_turned, key_turned)
    terms = exchanged(
        terms_of(turned, heads[2:], decay, carried, local_push, slope, layer_input)
    )
    grads = full_of(heads[1:], decay, carried, *local_parts)
    sums = after(jnp.sum(terms, axis=0), grads[0])
    token_count = BLOCK * lax.axis_size("seq") * lax.axis_size("dp")
    weight_grad = summed_over_dp(sums) / token_count
    return *grads, weight_grad


def solution(mesh):
    heads = P("dp", "seq", None)
    return jax.shard_map(
        local,
        mesh=mesh,
        in_specs=(heads,) * 5 + (P(), P("dp", None, "seq")),
        out_specs=(heads,) * 3 + (P(None, "seq"),),
        check_vma=False,
    )
```
